256 devices in a mesh: path: 64 (over y, z, core), dp: 4 (over x).
Axes of the slice: x: 4, y: 4, z: 8, core: 2. Of those that a mesh axis runs over, the one named last changes fastest.
Arguments:
- path_params: bfloat16 [128, 32, 8192], P('path', None, 'dp'), may hold values from -6 to 6
- path_module: int32 [128], replicated, may hold values from 0 to 15, as said below
- owner_of: int32 [16], replicated, may hold values from 0 to 63, as said below
- outer_params: float32 [64, 32, 8192], P('path', None, 'dp'), may hold values from -6 to 6
- momentum: float32 [64, 32, 8192], P('path', None, 'dp'), may hold values from -6 to 6
Outputs:
- new_outer: float32 [64, 32, 8192], P('path', None, 'dp')
- new_momentum: float32 [64, 32, 8192], P('path', None, 'dp')
- refreshed: bfloat16 [128, 32, 8192], P('path', None, 'dp')
The draws below stay inside these ranges and needn't reach their ends.
Inputs may be any that keep to these rules, and one draw needn't show every extreme that they name: `path_module`: every module is used by at least one path; counts are uneven. `owner_of`: distinct owner slots, one for each module.
All inputs are finite; a program needn't handle non-finite values.
Results may differ from the reference program's by a relative error of at most 0.0004.
Values may be sent and summed in bfloat16 or wider, within the bound.
A program may use at most 64 MiB of HBM per device.

```python
import jax
import jax.numpy as jnp
from jax import lax

MODULES = 16
FF = 8192
R = 32
OWNERS = 64
PATHS = 128


def draw_path_module(key, part):
    key = jax.random.fold_in(key, 11)
    first, second, third = jax.random.split(key, 3)
    left = jax.random.randint(first, (PATHS,), 0, MODULES)
    right = jax.random.randint(second, (PATHS,), 0, MODULES)
    chosen = jnp.minimum(left, right)
    order = jax.random.permutation(third, PATHS)
    return chosen.at[order[:MODULES]].set(jnp.arange(MODULES, dtype=jnp.int32)).astype(jnp.int32)


def draw_owner_of(key, part):
    key = jax.random.fold_in(key, 23)
    order = jax.random.permutation(key, OWNERS)
    return order[:MODULES].astype(jnp.int32)


def levels(stream_key, dims, cuts, smallest, largest):
    gain, own = 1.0, jax.random.fold_in(stream_key, 6)
    for position, shards_of in cuts:
        draws = jnp.exp(jax.random.uniform(jax.random.fold_in(own, position), (shards_of,), jnp.float32, smallest / len(cuts), largest / len(cuts)))
        gain = gain * jnp.repeat(draws, dims[position] // shards_of).reshape([-1 if axis == position else 1 for axis in range(len(dims))])
    return gain


def noise(key, extent, width, most, cuts=(), kind=jnp.bfloat16):
    drawn = jax.random.normal(key, extent, jnp.float32) * width
    if len(cuts) > 0:
        drawn = levels(key, extent, cuts, -0.22, 0.18) * drawn
    return jnp.clip(drawn, min=-most, max=most).astype(kind)


def setup_inputs(seed: int = 0) -> dict:
    key_of = jax.random.split(jax.random.key(seed), 6)
    path_params = noise(key_of[0], (PATHS, R, FF), 1.0, 6.0, ((0, 64), (2, 4)))
    path_module = draw_path_module(jax.random.fold_in(key_of[5], 71), 0)
    owner_of = draw_owner_of(jax.random.fold_in(key_of[5], 71), 0)
    outer_params = noise(key_of[3], (OWNERS, R, FF), 1.0, 6.0, ((0, 64), (2, 4)), jnp.float32)
    momentum = noise(key_of[4], (OWNERS, R, FF), 1.0, 6.0, ((0, 64), (2, 4)), jnp.float32)
    return {"path_params": path_params, "path_module": path_module, "owner_of": owner_of, "outer_params": outer_params, "momentum": momentum}


def reference(path_params, path_module, owner_of, outer_params, momentum):
    high = lax.Precision.HIGHEST
    values = path_params.astype(jnp.float32)
    onehot = (path_module[:, None] == jnp.arange(MODULES, dtype=jnp.int32)[None, :]).astype(jnp.float32)
    counts = lax.optimization_barrier(jnp.sum(onehot, axis=0))
    sums = jnp.einsum('pm,prc->mrc', onehot, values, precision=high)
    mean = sums / jnp.maximum(counts, 1.0)[:, None, None]
    owned = (owner_of[None, :] == jnp.arange(OWNERS, dtype=jnp.int32)[:, None]).astype(jnp.float32)
    held = lax.optimization_barrier(jnp.sum(owned, axis=1)) > 0.5
    mean_owned = jnp.einsum('om,mrc->orc', owned, mean, precision=high)
    pseudo = jnp.where(held[:, None, None], outer_params - mean_owned, 0.0)
    squares = lax.optimization_barrier(jnp.sum(pseudo * pseudo, axis=(1, 2)))
    limit = 0.5 * jnp.sqrt(jnp.float32(R * FF))
    factor = jnp.minimum(1.0, limit / jnp.sqrt(squares + 1e-06))
    grad = factor[:, None, None] * pseudo
    velocity = 0.9 * momentum + grad
    theta = outer_params - 0.7 * (0.9 * velocity + grad)
    new_outer = jnp.where(held[:, None, None], theta, outer_params)
    new_momentum = jnp.where(held[:, None, None], velocity, momentum)
    select = jnp.dot(onehot, owned.T, precision=high)
    refreshed = jnp.einsum('po,orc->prc', select, new_outer.astype(jnp.bfloat16).astype(jnp.float32), precision=high)
    return (new_outer, new_momentum, refreshed.astype(jnp.bfloat16))
```

```python
import jax
import jax.numpy as jnp
from jax import lax
from jax.sharding import PartitionSpec as P

FF = 8192
R = 32


def to_chunks(slab):
    n = slab.shape[0]
    return slab.reshape(n, 4, 8, 16, 128).transpose(1, 3, 0, 2, 4).reshape(64, n, 8, 128)


def from_chunks(chunks):
    n = chunks.shape[1]
    return chunks.reshape(4, 16, n, 8, 128).transpose(2, 0, 3, 1, 4).reshape(n, 32, 2048)


def exchange(chunks):
    return lax.all_to_all(chunks, "path", 0, 0, tiled=True)


def local(path_params, path_module, owner_of, outer_params, momentum):
    modules = owner_of.shape[0]
    group = lax.axis_index("path")
    module_ids = jnp.arange(modules, dtype=jnp.int32)
    slot_ids = jnp.arange(64, dtype=jnp.int32)
    slot_of_path = jnp.sum(
        jnp.where(path_module[:, None] == module_ids[None, :], owner_of[None, :], 0), axis=1
    )
    held = jnp.any(owner_of == group)
    hot = slot_of_path[None, :] == slot_ids[:, None]
    counts = jnp.sum(hot.astype(jnp.float32), axis=1)

    mine = exchange(to_chunks(path_params)).reshape(128, 1024)
    sums = jnp.dot(hot.astype(jnp.bfloat16), mine, preferred_element_type=jnp.float32)
    mean = sums / jnp.maximum(counts, 1.0)[:, None]
    mean = from_chunks(exchange(mean.reshape(64, 1, 8, 128)))

    pseudo = jnp.where(held, outer_params - mean, 0.0)
    squares = lax.psum(jnp.sum(pseudo * pseudo), "dp")
    limit = 0.5 * jnp.sqrt(jnp.float32(R * FF))
    factor = jnp.minimum(1.0, limit / jnp.sqrt(squares + 1e-06))
    grad = factor * pseudo
    velocity = 0.9 * momentum + grad
    theta = outer_params - 0.7 * (0.9 * velocity + grad)
    new_outer = jnp.where(held, theta, outer_params)
    new_momentum = jnp.where(held, velocity, momentum)

    slabs = exchange(to_chunks(new_outer.astype(jnp.bfloat16))).reshape(64, 1024)
    chosen = jnp.dot(hot.astype(jnp.bfloat16).T, slabs, preferred_element_type=jnp.float32)
    refreshed = from_chunks(exchange(chosen.astype(jnp.bfloat16).reshape(64, 2, 8, 128)))
    return (new_outer, new_momentum, refreshed)


def solution(mesh):
    return jax.shard_map(
        local,
        mesh=mesh,
        in_specs=(P("path", None, "dp"), P(), P(), P("path", None, "dp"), P("path", None, "dp")),
        out_specs=(P("path", None, "dp"), P("path", None, "dp"), P("path", None, "dp")),
        check_vma=False,
    )
```

```python
import jax
import jax.numpy as jnp
from jax import lax
from jax.experimental import pallas as pl
from jax.experimental.pallas import tpu as pltpu
from jax.sharding import PartitionSpec as P

FF = 8192
R = 32
MODULES = 16
N = 64
DP = 4
MESH = pl.DeviceIdType.MESH
F32 = jnp.float32
BF16 = jnp.bfloat16


def zig(j, middle):
    return middle + (1 - 2 * lax.rem(j, 2)) * lax.div(j + 1, 2)


def peer(me, k):
    y, z, core = lax.div(me, 16), lax.rem(lax.div(me, 2), 8), lax.rem(me, 2)
    dy = zig(lax.div(k, 16), 2)
    dz = zig(lax.rem(lax.div(k, 2), 8), 4)
    dc = 1 - lax.rem(k, 2)
    return lax.rem(y + dy, 4) * 16 + lax.rem(z + dz, 8) * 2 + lax.rem(core + dc, 2)


def rows(index, count):
    return pl.ds(pl.multiple_of(index * count, count), count)


def tile(index):
    return (rows(lax.div(index, 16), 8), rows(lax.rem(index, 16), 128))


def kernel(
    module_ref, owner_ref, x_hbm, outer_hbm, mom_hbm,
    new_outer_ref, new_mom_ref, fresh_ref,
    x_v, outer_v, mom_v, x_send, x_recv, outer_recv, mom_recv, mean_send, mean_slab,
    fresh_send, fresh_recv, dp_recv, vec_recv, weights, select,
    load_sem, send_sem, recv_sem,
):
    me = lax.axis_index("path")
    plane = lax.axis_index("dp")

    loads = [
        pltpu.make_async_copy(src.at[...], dst.at[...], load_sem.at[i])
        for i, (src, dst) in enumerate(((x_hbm, x_v), (outer_hbm, outer_v), (mom_hbm, mom_v)))
    ]
    for load in loads:
        load.start()

    barrier = pltpu.get_barrier_semaphore()

    @pl.loop(0, N - 1)
    def _(k):
        pl.semaphore_signal(barrier, inc=1, device_id={"path": peer(me, k)}, device_id_type=MESH)

    for k in range(1, DP):
        pl.semaphore_signal(
            barrier, inc=1, device_id={"dp": lax.rem(plane + k, DP)}, device_id_type=MESH
        )

    loads[0].wait()
    for half in range(2):
        first = x_v[0, 16 * half : 16 * half + 16, :].astype(F32)
        second = x_v[1, 16 * half : 16 * half + 16, :].astype(F32)
        for part in range(2):
            both = jnp.concatenate(
                [first[8 * part : 8 * part + 8], second[8 * part : 8 * part + 8]], axis=0
            ).astype(BF16)
            for column in range(16):
                chunk = (2 * half + part) * 16 + column
                x_send[16 * chunk : 16 * chunk + 16, :] = both[:, 128 * column : 128 * column + 128]
    loads[1].wait()
    loads[2].wait()

    pl.semaphore_wait(barrier, N - 1 + DP - 1)

    def send_all(stage, source, target):
        @pl.loop(0, N - 1)
        def _(k):
            to = peer(me, k)
            pltpu.make_async_remote_copy(
                src_ref=source(to), dst_ref=target, send_sem=send_sem.at[stage],
                recv_sem=recv_sem.at[stage], device_id={"path": to}, device_id_type=MESH,
            ).start()

    def wait(sem, ref, count):
        view = ref.at[pl.ds(0, count)]
        pltpu.make_async_copy(view, view, sem).wait()

    send_all(0, lambda to: x_send.at[rows(to, 16)], x_recv.at[rows(me, 16)])
    send_all(1, lambda to: outer_v.at[0].at[tile(to)], outer_recv.at[rows(me, 8)])
    send_all(2, lambda to: mom_v.at[0].at[tile(to)], mom_recv.at[rows(me, 8)])
    x_recv[rows(me, 16), :] = x_send[rows(me, 16), :]
    outer_recv[rows(me, 8), :] = outer_v[0, tile(me)[0], tile(me)[1]]
    mom_recv[rows(me, 8), :] = mom_v[0, tile(me)[0], tile(me)[1]]

    path_modules = jnp.broadcast_to(module_ref[...], (8, 128))
    slot_of_path = jnp.zeros((8, 128), jnp.int32)
    held_here = jnp.int32(0)
    for m in range(MODULES):
        owner = owner_ref[m]
        slot_of_path = jnp.where(path_modules == m, owner, slot_of_path)
        held_here = jnp.where(owner == me, 1, held_here)
    slot_of_path = slot_of_path.astype(F32)

    def iota(shape, axis):
        return lax.broadcasted_iota(jnp.int32, shape, axis)

    spread = (iota((128, 1024), 1) // 8 == iota((128, 1024), 0)).astype(F32).astype(BF16)
    across = jnp.dot(slot_of_path.astype(BF16), spread, preferred_element_type=F32)[0:1]
    shape = (N * 8, 1024)
    slot, row = (iota((N * 8, 1), 0) // 8).astype(F32), iota((N * 8, 1), 0) % 8
    hot = jnp.where((across == slot) & (iota((1, 1024), 1) % 8 == row), F32(1), F32(0))
    counts = jnp.sum(hot, axis=1, keepdims=True)
    weights[...] = hot.astype(BF16)
    down = jnp.sum(
        jnp.where(iota((1024, 128), 0) // 8 == iota((1024, 128), 1), slot_of_path[0:1], 0.0),
        axis=1, keepdims=True,
    )
    slot, row = (iota((1, N * 8), 1) // 8).astype(F32), iota((1, N * 8), 1) % 8
    select[...] = jnp.where(
        (down == slot) & (iota((1024, 1), 0) % 8 == row), F32(1), F32(0)
    ).astype(BF16)
    diagonal = iota((N * 8, 128), 0) // 8 == iota((N * 8, 128), 1)
    held = counts > 0.5
    divisor = jnp.maximum(counts, 1.0)

    wait(recv_sem.at[0], x_recv, 16 * (N - 1))
    sums = jnp.dot(weights[...], x_recv[...], preferred_element_type=F32)
    mean = sums / divisor
    mean_send[...] = mean
    wait(recv_sem.at[1], outer_recv, 8 * (N - 1))
    pseudo = jnp.where(held, outer_recv[...] - mean, 0.0)
    squares = jnp.sum(pseudo * pseudo, axis=1, keepdims=True)
    squares = jnp.sum(jnp.where(diagonal, squares, 0.0), axis=0, keepdims=True)

    dp_recv[pl.ds(plane, 1), :] = squares
    for k in range(1, DP):
        pltpu.make_async_remote_copy(
            src_ref=dp_recv.at[pl.ds(plane, 1)], dst_ref=dp_recv.at[pl.ds(plane, 1)],
            send_sem=send_sem.at[3], recv_sem=recv_sem.at[3],
            device_id={"dp": lax.rem(plane + k, DP)}, device_id_type=MESH,
        ).start()
    send_all(4, lambda to: mean_send.at[rows(to, 8)], mean_slab.at[tile(me)])
    mean_slab[tile(me)[0], tile(me)[1]] = mean_send[rows(me, 8), :]
    wait(recv_sem.at[3], dp_recv, DP - 1)
    everywhere = dp_recv[0:1] + dp_recv[1:2] + dp_recv[2:3] + dp_recv[3:4]

    vec_recv[pl.ds(me, 1), :] = everywhere
    send_all(5, lambda to: vec_recv.at[pl.ds(me, 1)], vec_recv.at[pl.ds(me, 1)])
    wait(recv_sem.at[2], mom_recv, 8 * (N - 1))
    limit = 0.5 * (float(R * FF) ** 0.5)
    wait(recv_sem.at[5], vec_recv, N - 1)
    total = jnp.sum(vec_recv[...], axis=0, keepdims=True)
    factors = jnp.minimum(1.0, limit / jnp.sqrt(total + 1e-06))

    factor = jnp.sum(jnp.where(diagonal, factors, 0.0), axis=1, keepdims=True)
    grad = factor * pseudo
    velocity = 0.9 * mom_recv[...] + grad
    theta = outer_recv[...] - 0.7 * (0.9 * velocity + grad)
    fresh_send[...] = jnp.dot(
        select[...], theta.astype(BF16), preferred_element_type=F32
    ).astype(BF16)
    send_all(6, lambda to: fresh_send.at[rows(to, 16)], fresh_recv.at[rows(me, 16)])
    fresh_recv[rows(me, 16), :] = fresh_send[rows(me, 16), :]

    held_slot = held_here > 0
    own_factor = jnp.sum(
        jnp.where(iota((1, 128), 1) == me, factors, 0.0), axis=1, keepdims=True
    )
    wait(recv_sem.at[4], mean_send, 8 * (N - 1))
    outer, mom = outer_v[0], mom_v[0]
    grad = own_factor * (outer - mean_slab[...])
    velocity = 0.9 * mom + grad
    theta = outer - 0.7 * (0.9 * velocity + grad)
    new_outer_ref[0] = jnp.where(held_slot, theta, outer)
    new_mom_ref[0] = jnp.where(held_slot, velocity, mom)

    wait(recv_sem.at[6], fresh_recv, 16 * (N - 1))
    for half in range(2):
        for column in range(16):
            top = fresh_recv[16 * (32 * half + column) : 16 * (32 * half + column) + 16, :].astype(F32)
            low = 16 * (32 * half + 16 + column)
            bottom = fresh_recv[low : low + 16, :].astype(F32)
            for path in range(2):
                fresh_ref[path, 16 * half : 16 * half + 16, 128 * column : 128 * column + 128] = (
                    jnp.concatenate(
                        [top[8 * path : 8 * path + 8], bottom[8 * path : 8 * path + 8]], axis=0
                    ).astype(BF16)
                )

    wait(send_sem.at[0], x_send, 16 * (N - 1))
    wait(send_sem.at[1], outer_recv, 8 * (N - 1))
    wait(send_sem.at[2], mom_recv, 8 * (N - 1))
    wait(send_sem.at[3], dp_recv, DP - 1)
    wait(send_sem.at[4], mean_send, 8 * (N - 1))
    wait(send_sem.at[5], vec_recv, N - 1)
    wait(send_sem.at[6], fresh_send, 16 * (N - 1))


def local(path_params, path_module, owner_of, outer_params, momentum):
    vmem = pl.BlockSpec(memory_space=pltpu.VMEM)
    anywhere = pl.BlockSpec(memory_space=pl.ANY)
    return pl.pallas_call(
        kernel,
        out_shape=(
            jax.ShapeDtypeStruct((1, R, 2048), F32),
            jax.ShapeDtypeStruct((1, R, 2048), F32),
            jax.ShapeDtypeStruct((2, R, 2048), BF16),
        ),
        in_specs=[vmem, pl.BlockSpec(memory_space=pltpu.SMEM), anywhere, anywhere, anywhere],
        out_specs=(vmem, vmem, vmem),
        scratch_shapes=[
            pltpu.VMEM((2, R, 2048), BF16),
            pltpu.VMEM((1, R, 2048), F32),
            pltpu.VMEM((1, R, 2048), F32),
            pltpu.VMEM((16 * N, 128), BF16),
            pltpu.VMEM((16 * N, 128), BF16),
            pltpu.VMEM((8 * N, 128), F32),
            pltpu.VMEM((8 * N, 128), F32),
            pltpu.VMEM((8 * N, 128), F32),
            pltpu.VMEM((R, 2048), F32),
            pltpu.VMEM((16 * N, 128), BF16),
            pltpu.VMEM((16 * N, 128), BF16),
            pltpu.VMEM((DP, 128), F32),
            pltpu.VMEM((N, 128), F32),
            pltpu.VMEM((8 * N, 1024), BF16),
            pltpu.VMEM((1024, 8 * N), BF16),
            pltpu.SemaphoreType.DMA((3,)),
            pltpu.SemaphoreType.DMA((7,)),
            pltpu.SemaphoreType.DMA((7,)),
        ],
        compiler_params=pltpu.CompilerParams(
            collective_id=0, has_side_effects=True, vmem_limit_bytes=48 << 20
        ),
    )(path_module.reshape(1, 128), owner_of, path_params, outer_params, momentum)


def solution(mesh):
    return jax.shard_map(
        local,
        mesh=mesh,
        in_specs=(P("path", None, "dp"), P(), P(), P("path", None, "dp"), P("path", None, "dp")),
        out_specs=(P("path", None, "dp"), P("path", None, "dp"), P("path", None, "dp")),
        check_vma=False,
    )
```

```python
import jax
import jax.numpy as jnp
from jax import lax
from jax.experimental import pallas as pl
from jax.experimental.pallas import tpu as pltpu
from jax.sharding import PartitionSpec as P

FF = 8192
R = 32
MODULES = 16
N = 64
DP = 4
MESH = pl.DeviceIdType.MESH
F32 = jnp.float32
BF16 = jnp.bfloat16


def zig(j, middle):
    return middle + (1 - 2 * lax.rem(j, 2)) * lax.div(j + 1, 2)


def peer(me, k):
    y, z, core = lax.div(me, 16), lax.rem(lax.div(me, 2), 8), lax.rem(me, 2)
    dy = zig(lax.div(k, 16), 2)
    dz = zig(lax.rem(lax.div(k, 2), 8), 4)
    dc = 1 - lax.rem(k, 2)
    return lax.rem(y + dy, 4) * 16 + lax.rem(z + dz, 8) * 2 + lax.rem(core + dc, 2)


def rows(index, count):
    return pl.ds(pl.multiple_of(index * count, count), count)


def tile(index):
    return (rows(lax.div(index, 16), 8), rows(lax.rem(index, 16), 128))


def kernel(
    module_hbm, owner_hbm, x_hbm, outer_hbm, mom_hbm,
    new_outer_ref, new_mom_ref, fresh_ref,
    module_ref, owner_ref, x_v, outer_v, mom_v, x_send, x_recv, outer_recv, mom_recv, mean_send, mean_slab,
    fresh_send, fresh_recv, dp_recv, vec_recv, weights, select,
    load_sem, send_sem, recv_sem,
):
    me = lax.axis_index("path")
    plane = lax.axis_index("dp")

    loads = [
        pltpu.make_async_copy(src, dst, load_sem.at[i])
        for i, (src, dst) in enumerate((
            (x_hbm, x_v), (outer_hbm, outer_v), (mom_hbm, mom_v),
            (module_hbm, module_ref), (owner_hbm, owner_ref),
        ))
    ]
    for load in loads:
        load.start()

    barrier = pltpu.get_barrier_semaphore()

    @pl.loop(0, N - 1)
    def _(k):
        pl.semaphore_signal(barrier, inc=1, device_id={"path": peer(me, k)}, device_id_type=MESH)

    for k in range(1, DP):
        pl.semaphore_signal(
            barrier, inc=1, device_id={"dp": lax.rem(plane + k, DP)}, device_id_type=MESH
        )

    loads[0].wait()
    for half in range(2):
        first = x_v[0, 16 * half : 16 * half + 16, :].astype(F32)
        second = x_v[1, 16 * half : 16 * half + 16, :].astype(F32)
        for part in range(2):
            both = jnp.concatenate(
                [first[8 * part : 8 * part + 8], second[8 * part : 8 * part + 8]], axis=0
            ).astype(BF16)
            for column in range(16):
                chunk = (2 * half + part) * 16 + column
                x_send[16 * chunk : 16 * chunk + 16, :] = both[:, 128 * column : 128 * column + 128]
    for load in loads[1:]:
        load.wait()

    pl.semaphore_wait(barrier, N - 1 + DP - 1)

    def send_all(stage, source, target):
        @pl.loop(0, N - 1)
        def _(k):
            to = peer(me, k)
            pltpu.make_async_remote_copy(
                src_ref=source(to), dst_ref=target, send_sem=send_sem.at[stage],
                recv_sem=recv_sem.at[stage], device_id={"path": to}, device_id_type=MESH,
            ).start()

    def wait(sem, ref, count):
        view = ref.at[pl.ds(0, count)]
        pltpu.make_async_copy(view, view, sem).wait()

    send_all(0, lambda to: x_send.at[rows(to, 16)], x_recv.at[rows(me, 16)])
    send_all(1, lambda to: outer_v.at[0].at[tile(to)], outer_recv.at[rows(me, 8)])
    send_all(2, lambda to: mom_v.at[0].at[tile(to)], mom_recv.at[rows(me, 8)])
    x_recv[rows(me, 16), :] = x_send[rows(me, 16), :]
    outer_recv[rows(me, 8), :] = outer_v[0, tile(me)[0], tile(me)[1]]
    mom_recv[rows(me, 8), :] = mom_v[0, tile(me)[0], tile(me)[1]]

    path_modules = jnp.broadcast_to(module_ref[...], (8, 128))
    slot_of_path = jnp.zeros((8, 128), jnp.int32)
    held_here = jnp.int32(0)
    for m in range(MODULES):
        owner = owner_ref[m]
        slot_of_path = jnp.where(path_modules == m, owner, slot_of_path)
        held_here = jnp.where(owner == me, 1, held_here)
    slot_of_path = slot_of_path.astype(F32)

    def iota(shape, axis):
        return lax.broadcasted_iota(jnp.int32, shape, axis)

    spread = (iota((128, 1024), 1) // 8 == iota((128, 1024), 0)).astype(F32).astype(BF16)
    across = jnp.dot(slot_of_path.astype(BF16), spread, preferred_element_type=F32)[0:1]
    shape = (N * 8, 1024)
    slot, row = (iota((N * 8, 1), 0) // 8).astype(F32), iota((N * 8, 1), 0) % 8
    hot = jnp.where((across == slot) & (iota((1, 1024), 1) % 8 == row), F32(1), F32(0))
    counts = jnp.sum(hot, axis=1, keepdims=True)
    weights[...] = hot.astype(BF16)
    down = jnp.sum(
        jnp.where(iota((1024, 128), 0) // 8 == iota((1024, 128), 1), slot_of_path[0:1], 0.0),
        axis=1, keepdims=True,
    )
    slot, row = (iota((1, N * 8), 1) // 8).astype(F32), iota((1, N * 8), 1) % 8
    select[...] = jnp.where(
        (down == slot) & (iota((1024, 1), 0) % 8 == row), F32(1), F32(0)
    ).astype(BF16)
    diagonal = iota((N * 8, 128), 0) // 8 == iota((N * 8, 128), 1)
    held = counts > 0.5
    divisor = jnp.maximum(counts, 1.0)

    wait(recv_sem.at[0], x_recv, 16 * (N - 1))
    sums = jnp.dot(weights[...], x_recv[...], preferred_element_type=F32)
    mean = sums / divisor
    mean_send[...] = mean
    wait(recv_sem.at[1], outer_recv, 8 * (N - 1))
    pseudo = jnp.where(held, outer_recv[...] - mean, 0.0)
    squares = jnp.sum(pseudo * pseudo, axis=1, keepdims=True)
    squares = jnp.sum(jnp.where(diagonal, squares, 0.0), axis=0, keepdims=True)

    dp_recv[pl.ds(plane, 1), :] = squares
    for k in range(1, DP):
        pltpu.make_async_remote_copy(
            src_ref=dp_recv.at[pl.ds(plane, 1)], dst_ref=dp_recv.at[pl.ds(plane, 1)],
            send_sem=send_sem.at[3], recv_sem=recv_sem.at[3],
            device_id={"dp": lax.rem(plane + k, DP)}, device_id_type=MESH,
        ).start()
    send_all(4, lambda to: mean_send.at[rows(to, 8)], mean_slab.at[tile(me)])
    mean_slab[tile(me)[0], tile(me)[1]] = mean_send[rows(me, 8), :]
    wait(recv_sem.at[3], dp_recv, DP - 1)
    everywhere = dp_recv[0:1] + dp_recv[1:2] + dp_recv[2:3] + dp_recv[3:4]

    vec_recv[pl.ds(me, 1), :] = everywhere
    send_all(5, lambda to: vec_recv.at[pl.ds(me, 1)], vec_recv.at[pl.ds(me, 1)])
    wait(recv_sem.at[2], mom_recv, 8 * (N - 1))
    limit = 0.5 * (float(R * FF) ** 0.5)
    wait(recv_sem.at[5], vec_recv, N - 1)
    total = jnp.sum(vec_recv[...], axis=0, keepdims=True)
    factors = jnp.minimum(1.0, limit / jnp.sqrt(total + 1e-06))

    factor = jnp.sum(jnp.where(diagonal, factors, 0.0), axis=1, keepdims=True)
    grad = factor * pseudo
    velocity = 0.9 * mom_recv[...] + grad
    theta = outer_recv[...] - 0.7 * (0.9 * velocity + grad)
    fresh_send[...] = jnp.dot(
        select[...], theta.astype(BF16), preferred_element_type=F32
    ).astype(BF16)
    send_all(6, lambda to: fresh_send.at[rows(to, 16)], fresh_recv.at[rows(me, 16)])
    fresh_recv[rows(me, 16), :] = fresh_send[rows(me, 16), :]

    held_slot = held_here > 0
    own_factor = jnp.sum(
        jnp.where(iota((1, 128), 1) == me, factors, 0.0), axis=1, keepdims=True
    )
    wait(recv_sem.at[4], mean_send, 8 * (N - 1))
    outer, mom = outer_v[0], mom_v[0]
    grad = own_factor * (outer - mean_slab[...])
    velocity = 0.9 * mom + grad
    theta = outer - 0.7 * (0.9 * velocity + grad)
    new_outer_ref[0] = jnp.where(held_slot, theta, outer)
    new_mom_ref[0] = jnp.where(held_slot, velocity, mom)

    wait(recv_sem.at[6], fresh_recv, 16 * (N - 1))
    for half in range(2):
        for column in range(16):
            top = fresh_recv[16 * (32 * half + column) : 16 * (32 * half + column) + 16, :].astype(F32)
            low = 16 * (32 * half + 16 + column)
            bottom = fresh_recv[low : low + 16, :].astype(F32)
            for path in range(2):
                fresh_ref[path, 16 * half : 16 * half + 16, 128 * column : 128 * column + 128] = (
                    jnp.concatenate(
                        [top[8 * path : 8 * path + 8], bottom[8 * path : 8 * path + 8]], axis=0
                    ).astype(BF16)
                )

    wait(send_sem.at[0], x_send, 16 * (N - 1))
    wait(send_sem.at[1], outer_recv, 8 * (N - 1))
    wait(send_sem.at[2], mom_recv, 8 * (N - 1))
    wait(send_sem.at[3], dp_recv, DP - 1)
    wait(send_sem.at[4], mean_send, 8 * (N - 1))
    wait(send_sem.at[5], vec_recv, N - 1)
    wait(send_sem.at[6], fresh_send, 16 * (N - 1))


def write_out(a_ref, b_ref, c_ref, a_hbm, b_hbm, c_hbm, sem):
    copies = [
        pltpu.make_async_copy(src, dst, sem.at[i])
        for i, (src, dst) in enumerate(((a_ref, a_hbm), (b_ref, b_hbm), (c_ref, c_hbm)))
    ]
    for copy in copies:
        copy.start()
    for copy in copies:
        copy.wait()


def local(path_params, path_module, owner_of, outer_params, momentum):
    vmem = pl.BlockSpec(memory_space=pltpu.VMEM)
    hbm = pl.BlockSpec(memory_space=pl.ANY)
    shapes = (
        jax.ShapeDtypeStruct((1, R, 2048), F32),
        jax.ShapeDtypeStruct((1, R, 2048), F32),
        jax.ShapeDtypeStruct((2, R, 2048), BF16),
    )
    results = pl.pallas_call(
        kernel,
        out_shape=shapes,
        in_specs=[hbm] * 5,
        out_specs=(vmem, vmem, vmem),
        scratch_shapes=[
            pltpu.VMEM((1, 128), jnp.int32),
            pltpu.SMEM((MODULES,), jnp.int32),
            pltpu.VMEM((2, R, 2048), BF16),
            pltpu.VMEM((1, R, 2048), F32),
            pltpu.VMEM((1, R, 2048), F32),
            pltpu.VMEM((16 * N, 128), BF16),
            pltpu.VMEM((16 * N, 128), BF16),
            pltpu.VMEM((8 * N, 128), F32),
            pltpu.VMEM((8 * N, 128), F32),
            pltpu.VMEM((8 * N, 128), F32),
            pltpu.VMEM((R, 2048), F32),
            pltpu.VMEM((16 * N, 128), BF16),
            pltpu.VMEM((16 * N, 128), BF16),
            pltpu.VMEM((DP, 128), F32),
            pltpu.VMEM((N, 128), F32),
            pltpu.VMEM((8 * N, 1024), BF16),
            pltpu.VMEM((1024, 8 * N), BF16),
            pltpu.SemaphoreType.DMA((5,)),
            pltpu.SemaphoreType.DMA((7,)),
            pltpu.SemaphoreType.DMA((7,)),
        ],
        compiler_params=pltpu.CompilerParams(
            collective_id=0, has_side_effects=True, vmem_limit_bytes=53 << 20
        ),
    )(path_module.reshape(1, 128), owner_of, path_params, outer_params, momentum)
    return pl.pallas_call(
        write_out,
        out_shape=shapes,
        in_specs=[hbm] * 3,
        out_specs=(hbm,) * 3,
        scratch_shapes=[pltpu.SemaphoreType.DMA((3,))],
        compiler_params=pltpu.CompilerParams(vmem_limit_bytes=1 << 20),
    )(*results)


def solution(mesh):
    return jax.shard_map(
        local,
        mesh=mesh,
        in_specs=(P("path", None, "dp"), P(), P(), P("path", None, "dp"), P("path", None, "dp")),
        out_specs=(P("path", None, "dp"), P("path", None, "dp"), P("path", None, "dp")),
        check_vma=False,
    )
```

```python
import jax
import jax.numpy as jnp
from jax import lax
from jax.experimental import pallas as pl
from jax.experimental.pallas import tpu as pltpu
from jax.sharding import PartitionSpec as P

FF = 8192
R = 32
MODULES = 16
N = 64
DP = 4
MESH = pl.DeviceIdType.MESH
F32 = jnp.float32
BF16 = jnp.bfloat16


def zig(j, middle):
    return middle + (1 - 2 * lax.rem(j, 2)) * lax.div(j + 1, 2)


def peer(me, k):
    y, z, core = lax.div(me, 16), lax.rem(lax.div(me, 2), 8), lax.rem(me, 2)
    dy = zig(lax.div(k, 16), 2)
    dz = zig(lax.rem(lax.div(k, 2), 8), 4)
    dc = 1 - lax.rem(k, 2)
    return lax.rem(y + dy, 4) * 16 + lax.rem(z + dz, 8) * 2 + lax.rem(core + dc, 2)


def rows(index, count):
    return pl.ds(pl.multiple_of(index * count, count), count)


def tile(index):
    return (rows(lax.div(index, 16), 8), rows(lax.rem(index, 16), 128))


def kernel(
    module_hbm, owner_hbm, x_hbm, outer_hbm, mom_hbm,
    new_outer_ref, new_mom_ref, fresh_ref,
    module_ref, owner_ref, x_v, outer_v, mom_v, x_send, x_recv, outer_recv, mom_recv, mean_send, mean_slab,
    fresh_send, fresh_recv, dp_recv, vec_recv, weights, select,
    load_sem, send_sem, recv_sem,
):
    me = lax.axis_index("path")
    plane = lax.axis_index("dp")

    loads = [
        pltpu.make_async_copy(src, dst, load_sem.at[i])
        for i, (src, dst) in enumerate((
            (x_hbm, x_v), (outer_hbm, outer_v), (mom_hbm, mom_v),
            (module_hbm, module_ref), (owner_hbm, owner_ref),
        ))
    ]
    for load in loads:
        load.start()

    barrier = pltpu.get_barrier_semaphore()

    @pl.loop(0, N - 1)
    def _(k):
        pl.semaphore_signal(barrier, inc=1, device_id={"path": peer(me, k)}, device_id_type=MESH)

    for k in range(1, DP):
        pl.semaphore_signal(
            barrier, inc=1, device_id={"dp": lax.rem(plane + k, DP)}, device_id_type=MESH
        )

    loads[0].wait()
    for half in range(2):
        first = x_v[0, 16 * half : 16 * half + 16, :].astype(F32)
        second = x_v[1, 16 * half : 16 * half + 16, :].astype(F32)
        for part in range(2):
            both = jnp.concatenate(
                [first[8 * part : 8 * part + 8], second[8 * part : 8 * part + 8]], axis=0
            ).astype(BF16)
            for column in range(16):
                chunk = (2 * half + part) * 16 + column
                x_send[16 * chunk : 16 * chunk + 16, :] = both[:, 128 * column : 128 * column + 128]
    for load in loads[1:]:
        load.wait()

    pl.semaphore_wait(barrier, N - 1 + DP - 1)

    def send_all(stage, source, target):
        @pl.loop(0, N - 1)
        def _(k):
            to = peer(me, k)
            pltpu.make_async_remote_copy(
                src_ref=source(to), dst_ref=target, send_sem=send_sem.at[stage],
                recv_sem=recv_sem.at[stage], device_id={"path": to}, device_id_type=MESH,
            ).start()

    def send_early(stage, source, target):
        @pl.loop(0, N)
        def _(k):
            i = lax.rem(k, 8)
            y, core = lax.div(me, 16), lax.rem(me, 2)
            z = lax.div(k, 8)
            to = (
                lax.rem(y + zig(lax.div(i, 2), 2), 4) * 16
                + z * 2
                + lax.rem(core + 1 - lax.rem(i, 2), 2)
            )

            @pl.when(to != me)
            def _():
                pltpu.make_async_remote_copy(
                    src_ref=source(to), dst_ref=target, send_sem=send_sem.at[stage],
                    recv_sem=recv_sem.at[stage], device_id={"path": to}, device_id_type=MESH,
                ).start()

    def wait(sem, ref, count):
        view = ref.at[pl.ds(0, count)]
        pltpu.make_async_copy(view, view, sem).wait()

    send_all(0, lambda to: x_send.at[rows(to, 16)], x_recv.at[rows(me, 16)])
    send_all(1, lambda to: outer_v.at[0].at[tile(to)], outer_recv.at[rows(me, 8)])
    send_all(2, lambda to: mom_v.at[0].at[tile(to)], mom_recv.at[rows(me, 8)])
    x_recv[rows(me, 16), :] = x_send[rows(me, 16), :]
    outer_recv[rows(me, 8), :] = outer_v[0, tile(me)[0], tile(me)[1]]
    mom_recv[rows(me, 8), :] = mom_v[0, tile(me)[0], tile(me)[1]]

    path_modules = jnp.broadcast_to(module_ref[...], (8, 128))
    slot_of_path = jnp.zeros((8, 128), jnp.int32)
    held_here = jnp.int32(0)
    for m in range(MODULES):
        owner = owner_ref[m]
        slot_of_path = jnp.where(path_modules == m, owner, slot_of_path)
        held_here = jnp.where(owner == me, 1, held_here)
    slot_of_path = slot_of_path.astype(F32)

    def iota(shape, axis):
        return lax.broadcasted_iota(jnp.int32, shape, axis)

    spread = (iota((128, 1024), 1) // 8 == iota((128, 1024), 0)).astype(F32).astype(BF16)
    across = jnp.dot(slot_of_path.astype(BF16), spread, preferred_element_type=F32)[0:1]
    shape = (N * 8, 1024)
    slot, row = (iota((N * 8, 1), 0) // 8).astype(F32), iota((N * 8, 1), 0) % 8
    hot = jnp.where((across == slot) & (iota((1, 1024), 1) % 8 == row), F32(1), F32(0))
    counts = jnp.sum(hot, axis=1, keepdims=True)
    weights[...] = hot.astype(BF16)
    down = jnp.sum(
        jnp.where(iota((1024, 128), 0) // 8 == iota((1024, 128), 1), slot_of_path[0:1], 0.0),
        axis=1, keepdims=True,
    )
    slot, row = (iota((1, N * 8), 1) // 8).astype(F32), iota((1, N * 8), 1) % 8
    select[...] = jnp.where(
        (down == slot) & (iota((1024, 1), 0) % 8 == row), F32(1), F32(0)
    ).astype(BF16)
    diagonal = iota((N * 8, 128), 0) // 8 == iota((N * 8, 128), 1)
    held = counts > 0.5
    divisor = jnp.maximum(counts, 1.0)

    wait(recv_sem.at[0], x_recv, 16 * (N - 1))
    sums = jnp.dot(weights[...], x_recv[...], preferred_element_type=F32)
    mean = sums / divisor
    mean_send[...] = mean
    wait(recv_sem.at[1], outer_recv, 8 * (N - 1))
    pseudo = jnp.where(held, outer_recv[...] - mean, 0.0)
    squares = jnp.sum(pseudo * pseudo, axis=1, keepdims=True)
    squares = jnp.sum(jnp.where(diagonal, squares, 0.0), axis=0, keepdims=True)

    dp_recv[pl.ds(plane, 1), :] = squares
    for k in range(1, DP):
        pltpu.make_async_remote_copy(
            src_ref=dp_recv.at[pl.ds(plane, 1)], dst_ref=dp_recv.at[pl.ds(plane, 1)],
            send_sem=send_sem.at[3], recv_sem=recv_sem.at[3],
            device_id={"dp": lax.rem(plane + k, DP)}, device_id_type=MESH,
        ).start()
    wait(recv_sem.at[3], dp_recv, DP - 1)
    everywhere = dp_recv[0:1] + dp_recv[1:2] + dp_recv[2:3] + dp_recv[3:4]

    vec_recv[pl.ds(me, 1), :] = everywhere
    send_all(5, lambda to: vec_recv.at[pl.ds(me, 1)], vec_recv.at[pl.ds(me, 1)])
    send_all(4, lambda to: mean_send.at[rows(to, 8)], mean_slab.at[tile(me)])
    mean_slab[tile(me)[0], tile(me)[1]] = mean_send[rows(me, 8), :]
    wait(recv_sem.at[2], mom_recv, 8 * (N - 1))
    limit = 0.5 * (float(R * FF) ** 0.5)
    wait(recv_sem.at[5], vec_recv, N - 1)
    total = jnp.sum(vec_recv[...], axis=0, keepdims=True)
    factors = jnp.minimum(1.0, limit / jnp.sqrt(total + 1e-06))

    factor = jnp.sum(jnp.where(diagonal, factors, 0.0), axis=1, keepdims=True)
    grad = factor * pseudo
    velocity = 0.9 * mom_recv[...] + grad
    theta = outer_recv[...] - 0.7 * (0.9 * velocity + grad)
    fresh_send[...] = jnp.dot(
        select[...], theta.astype(BF16), preferred_element_type=F32
    ).astype(BF16)
    send_early(6, lambda to: fresh_send.at[rows(to, 16)], fresh_recv.at[rows(me, 16)])
    fresh_recv[rows(me, 16), :] = fresh_send[rows(me, 16), :]

    held_slot = held_here > 0
    own_factor = jnp.sum(
        jnp.where(iota((1, 128), 1) == me, factors, 0.0), axis=1, keepdims=True
    )
    wait(recv_sem.at[4], mean_send, 8 * (N - 1))
    outer, mom = outer_v[0], mom_v[0]
    grad = own_factor * (outer - mean_slab[...])
    velocity = 0.9 * mom + grad
    theta = outer - 0.7 * (0.9 * velocity + grad)
    new_outer_ref[0] = jnp.where(held_slot, theta, outer)
    new_mom_ref[0] = jnp.where(held_slot, velocity, mom)

    wait(recv_sem.at[6], fresh_recv, 16 * (N - 1))
    for half in range(2):
        for column in range(16):
            top = fresh_recv[16 * (32 * half + column) : 16 * (32 * half + column) + 16, :].astype(F32)
            low = 16 * (32 * half + 16 + column)
            bottom = fresh_recv[low : low + 16, :].astype(F32)
            for path in range(2):
                fresh_ref[path, 16 * half : 16 * half + 16, 128 * column : 128 * column + 128] = (
                    jnp.concatenate(
                        [top[8 * path : 8 * path + 8], bottom[8 * path : 8 * path + 8]], axis=0
                    ).astype(BF16)
                )

    wait(send_sem.at[0], x_send, 16 * (N - 1))
    wait(send_sem.at[1], outer_recv, 8 * (N - 1))
    wait(send_sem.at[2], mom_recv, 8 * (N - 1))
    wait(send_sem.at[3], dp_recv, DP - 1)
    wait(send_sem.at[4], mean_send, 8 * (N - 1))
    wait(send_sem.at[5], vec_recv, N - 1)
    wait(send_sem.at[6], fresh_send, 16 * (N - 1))


def write_out(a_ref, b_ref, c_ref, a_hbm, b_hbm, c_hbm, sem):
    copies = [
        pltpu.make_async_copy(src, dst, sem.at[i])
        for i, (src, dst) in enumerate(((a_ref, a_hbm), (b_ref, b_hbm), (c_ref, c_hbm)))
    ]
    for copy in copies:
        copy.start()
    for copy in copies:
        copy.wait()


def local(path_params, path_module, owner_of, outer_params, momentum):
    vmem = pl.BlockSpec(memory_space=pltpu.VMEM)
    hbm = pl.BlockSpec(memory_space=pl.ANY)
    shapes = (
        jax.ShapeDtypeStruct((1, R, 2048), F32),
        jax.ShapeDtypeStruct((1, R, 2048), F32),
        jax.ShapeDtypeStruct((2, R, 2048), BF16),
    )
    results = pl.pallas_call(
        kernel,
        out_shape=shapes,
        in_specs=[hbm] * 5,
        out_specs=(vmem, vmem, vmem),
        scratch_shapes=[
            pltpu.VMEM((1, 128), jnp.int32),
            pltpu.SMEM((MODULES,), jnp.int32),
            pltpu.VMEM((2, R, 2048), BF16),
            pltpu.VMEM((1, R, 2048), F32),
            pltpu.VMEM((1, R, 2048), F32),
            pltpu.VMEM((16 * N, 128), BF16),
            pltpu.VMEM((16 * N, 128), BF16),
            pltpu.VMEM((8 * N, 128), F32),
            pltpu.VMEM((8 * N, 128), F32),
            pltpu.VMEM((8 * N, 128), F32),
            pltpu.VMEM((R, 2048), F32),
            pltpu.VMEM((16 * N, 128), BF16),
            pltpu.VMEM((16 * N, 128), BF16),
            pltpu.VMEM((DP, 128), F32),
            pltpu.VMEM((N, 128), F32),
            pltpu.VMEM((8 * N, 1024), BF16),
            pltpu.VMEM((1024, 8 * N), BF16),
            pltpu.SemaphoreType.DMA((5,)),
            pltpu.SemaphoreType.DMA((7,)),
            pltpu.SemaphoreType.DMA((7,)),
        ],
        compiler_params=pltpu.CompilerParams(
            collective_id=0, has_side_effects=True, vmem_limit_bytes=53 << 20
        ),
    )(path_module.reshape(1, 128), owner_of, path_params, outer_params, momentum)
    return pl.pallas_call(
        write_out,
        out_shape=shapes,
        in_specs=[hbm] * 3,
        out_specs=(hbm,) * 3,
        scratch_shapes=[pltpu.SemaphoreType.DMA((3,))],
        compiler_params=pltpu.CompilerParams(vmem_limit_bytes=1 << 20),
    )(*results)


def solution(mesh):
    return jax.shard_map(
        local,
        mesh=mesh,
        in_specs=(P("path", None, "dp"), P(), P(), P("path", None, "dp"), P("path", None, "dp")),
        out_specs=(P("path", None, "dp"), P("path", None, "dp"), P("path", None, "dp")),
        check_vma=False,
    )
```

```python
import jax
import jax.numpy as jnp
from jax import lax
from jax.experimental import pallas as pl
from jax.experimental.pallas import tpu as pltpu
from jax.sharding import PartitionSpec as P

FF = 8192
R = 32
MODULES = 16
N = 64
DP = 4
MESH = pl.DeviceIdType.MESH
F32 = jnp.float32
BF16 = jnp.bfloat16


def zig(j, middle):
    return middle + (1 - 2 * lax.rem(j, 2)) * lax.div(j + 1, 2)


def peer(me, k):
    y, z, core = lax.div(me, 16), lax.rem(lax.div(me, 2), 8), lax.rem(me, 2)
    dy = zig(lax.div(k, 16), 2)
    dz = zig(lax.rem(lax.div(k, 2), 8), 4)
    dc = 1 - lax.rem(k, 2)
    return lax.rem(y + dy, 4) * 16 + lax.rem(z + dz, 8) * 2 + lax.rem(core + dc, 2)


def rows(index, count):
    return pl.ds(pl.multiple_of(index * count, count), count)


def tile(index):
    return (rows(lax.div(index, 16), 8), rows(lax.rem(index, 16), 128))


def kernel(
    module_hbm, owner_hbm, x_hbm, outer_hbm, mom_hbm,
    new_outer_ref, new_mom_ref, fresh_ref,
    module_ref, owner_ref, x_v, outer_v, mom_v, x_send, x_recv, outer_recv, mom_recv, mean_send, mean_slab,
    fresh_send, fresh_recv, dp_recv, vec_recv, weights, select,
    load_sem, send_sem, recv_sem,
):
    me = lax.axis_index("path")
    plane = lax.axis_index("dp")

    loads = [
        pltpu.make_async_copy(src, dst, load_sem.at[i])
        for i, (src, dst) in enumerate((
            (x_hbm, x_v), (outer_hbm, outer_v), (mom_hbm, mom_v),
            (module_hbm, module_ref), (owner_hbm, owner_ref),
        ))
    ]
    for load in loads:
        load.start()

    barrier = pltpu.get_barrier_semaphore()

    @pl.loop(0, N - 1, unroll=3)
    def _(k):
        pl.semaphore_signal(barrier, inc=1, device_id={"path": peer(me, k)}, device_id_type=MESH)

    for k in range(1, DP):
        pl.semaphore_signal(
            barrier, inc=1, device_id={"dp": lax.rem(plane + k, DP)}, device_id_type=MESH
        )

    loads[0].wait()
    for half in range(2):
        first = x_v[0, 16 * half : 16 * half + 16, :].astype(F32)
        second = x_v[1, 16 * half : 16 * half + 16, :].astype(F32)
        for part in range(2):
            both = jnp.concatenate(
                [first[8 * part : 8 * part + 8], second[8 * part : 8 * part + 8]], axis=0
            ).astype(BF16)
            for column in range(16):
                chunk = (2 * half + part) * 16 + column
                x_send[16 * chunk : 16 * chunk + 16, :] = both[:, 128 * column : 128 * column + 128]
    for load in loads[1:]:
        load.wait()

    pl.semaphore_wait(barrier, N - 1 + DP - 1)

    def send_all(stage, source, target):
        @pl.loop(0, N - 1, unroll=3)
        def _(k):
            to = peer(me, k)
            pltpu.make_async_remote_copy(
                src_ref=source(to), dst_ref=target, send_sem=send_sem.at[stage],
                recv_sem=recv_sem.at[stage], device_id={"path": to}, device_id_type=MESH,
            ).start()

    def send_early(stage, source, target):
        @pl.loop(0, N, unroll=2)
        def _(k):
            y, z, core = lax.div(me, 16), lax.rem(lax.div(me, 2), 8), lax.rem(me, 2)
            dy, dz, dc = lax.rem(lax.div(k, 8), 4), lax.rem(lax.div(k, 2), 4), lax.rem(k, 2)
            to = dy * 16 + (lax.div(k, 32) * 4 + lax.rem(z + dz, 4)) * 2 + lax.rem(core + dc, 2)

            @pl.when(to != me)
            def _():
                pltpu.make_async_remote_copy(
                    src_ref=source(to), dst_ref=target, send_sem=send_sem.at[stage],
                    recv_sem=recv_sem.at[stage], device_id={"path": to}, device_id_type=MESH,
                ).start()

    def wait(sem, ref, count):
        view = ref.at[pl.ds(0, count)]
        pltpu.make_async_copy(view, view, sem).wait()

    send_all(0, lambda to: x_send.at[rows(to, 16)], x_recv.at[rows(me, 16)])
    send_all(1, lambda to: outer_v.at[0].at[tile(to)], outer_recv.at[rows(me, 8)])
    send_all(2, lambda to: mom_v.at[0].at[tile(to)], mom_recv.at[rows(me, 8)])
    x_recv[rows(me, 16), :] = x_send[rows(me, 16), :]
    outer_recv[rows(me, 8), :] = outer_v[0, tile(me)[0], tile(me)[1]]
    mom_recv[rows(me, 8), :] = mom_v[0, tile(me)[0], tile(me)[1]]

    path_modules = jnp.broadcast_to(module_ref[...], (8, 128))
    slot_of_path = jnp.zeros((8, 128), jnp.int32)
    held_here = jnp.int32(0)
    for m in range(MODULES):
        owner = owner_ref[m]
        slot_of_path = jnp.where(path_modules == m, owner, slot_of_path)
        held_here = jnp.where(owner == me, 1, held_here)
    slot_of_path = slot_of_path.astype(F32)

    def iota(shape, axis):
        return lax.broadcasted_iota(jnp.int32, shape, axis)

    spread = (iota((128, 1024), 1) // 8 == iota((128, 1024), 0)).astype(F32).astype(BF16)
    across = jnp.dot(slot_of_path.astype(BF16), spread, preferred_element_type=F32)[0:1]
    shape = (N * 8, 1024)
    slot, row = (iota((N * 8, 1), 0) // 8).astype(F32), iota((N * 8, 1), 0) % 8
    hot = jnp.where((across == slot) & (iota((1, 1024), 1) % 8 == row), F32(1), F32(0))
    counts = jnp.sum(hot, axis=1, keepdims=True)
    weights[...] = hot.astype(BF16)
    down = jnp.sum(
        jnp.where(iota((1024, 128), 0) // 8 == iota((1024, 128), 1), slot_of_path[0:1], 0.0),
        axis=1, keepdims=True,
    )
    slot, row = (iota((1, N * 8), 1) // 8).astype(F32), iota((1, N * 8), 1) % 8
    select[...] = jnp.where(
        (down == slot) & (iota((1024, 1), 0) % 8 == row), F32(1), F32(0)
    ).astype(BF16)
    diagonal = iota((N * 8, 128), 0) // 8 == iota((N * 8, 128), 1)
    held = counts > 0.5
    divisor = jnp.maximum(counts, 1.0)

    wait(recv_sem.at[0], x_recv, 16 * (N - 1))
    sums = jnp.dot(weights[...], x_recv[...], preferred_element_type=F32)
    mean = sums / divisor
    mean_send[...] = mean
    wait(recv_sem.at[1], outer_recv, 8 * (N - 1))
    pseudo = jnp.where(held, outer_recv[...] - mean, 0.0)
    squares = jnp.sum(pseudo * pseudo, axis=1, keepdims=True)
    squares = jnp.sum(jnp.where(diagonal, squares, 0.0), axis=0, keepdims=True)

    dp_recv[pl.ds(plane, 1), :] = squares
    for k in range(1, DP):
        pltpu.make_async_remote_copy(
            src_ref=dp_recv.at[pl.ds(plane, 1)], dst_ref=dp_recv.at[pl.ds(plane, 1)],
            send_sem=send_sem.at[3], recv_sem=recv_sem.at[3],
            device_id={"dp": lax.rem(plane + k, DP)}, device_id_type=MESH,
        ).start()
    wait(recv_sem.at[3], dp_recv, DP - 1)
    everywhere = dp_recv[0:1] + dp_recv[1:2] + dp_recv[2:3] + dp_recv[3:4]

    vec_recv[pl.ds(me, 1), :] = everywhere
    send_all(5, lambda to: vec_recv.at[pl.ds(me, 1)], vec_recv.at[pl.ds(me, 1)])
    send_all(4, lambda to: mean_send.at[rows(to, 8)], mean_slab.at[tile(me)])
    mean_slab[tile(me)[0], tile(me)[1]] = mean_send[rows(me, 8), :]
    wait(recv_sem.at[2], mom_recv, 8 * (N - 1))
    limit = 0.5 * (float(R * FF) ** 0.5)
    wait(recv_sem.at[5], vec_recv, N - 1)
    total = jnp.sum(vec_recv[...], axis=0, keepdims=True)
    factors = jnp.minimum(1.0, limit / jnp.sqrt(total + 1e-06))

    factor = jnp.sum(jnp.where(diagonal, factors, 0.0), axis=1, keepdims=True)
    grad = factor * pseudo
    velocity = 0.9 * mom_recv[...] + grad
    theta = outer_recv[...] - 0.7 * (0.9 * velocity + grad)
    fresh_send[...] = jnp.dot(
        select[...], theta.astype(BF16), preferred_element_type=F32
    ).astype(BF16)
    send_early(6, lambda to: fresh_send.at[rows(to, 16)], fresh_recv.at[rows(me, 16)])
    fresh_recv[rows(me, 16), :] = fresh_send[rows(me, 16), :]

    held_slot = held_here > 0
    own_factor = jnp.sum(
        jnp.where(iota((1, 128), 1) == me, factors, 0.0), axis=1, keepdims=True
    )
    wait(recv_sem.at[4], mean_send, 8 * (N - 1))
    outer, mom = outer_v[0], mom_v[0]
    grad = own_factor * (outer - mean_slab[...])
    velocity = 0.9 * mom + grad
    theta = outer - 0.7 * (0.9 * velocity + grad)
    new_outer_ref[0] = jnp.where(held_slot, theta, outer)
    new_mom_ref[0] = jnp.where(held_slot, velocity, mom)

    wait(recv_sem.at[6], fresh_recv, 16 * (N - 1))
    for half in range(2):
        for column in range(16):
            top = fresh_recv[16 * (32 * half + column) : 16 * (32 * half + column) + 16, :].astype(F32)
            low = 16 * (32 * half + 16 + column)
            bottom = fresh_recv[low : low + 16, :].astype(F32)
            for path in range(2):
                fresh_ref[path, 16 * half : 16 * half + 16, 128 * column : 128 * column + 128] = (
                    jnp.concatenate(
                        [top[8 * path : 8 * path + 8], bottom[8 * path : 8 * path + 8]], axis=0
                    ).astype(BF16)
                )

    wait(send_sem.at[0], x_send, 16 * (N - 1))
    wait(send_sem.at[1], outer_recv, 8 * (N - 1))
    wait(send_sem.at[2], mom_recv, 8 * (N - 1))
    wait(send_sem.at[3], dp_recv, DP - 1)
    wait(send_sem.at[4], mean_send, 8 * (N - 1))
    wait(send_sem.at[5], vec_recv, N - 1)
    wait(send_sem.at[6], fresh_send, 16 * (N - 1))


def write_out(a_ref, b_ref, c_ref, a_hbm, b_hbm, c_hbm, sem):
    copies = [
        pltpu.make_async_copy(src, dst, sem.at[i])
        for i, (src, dst) in enumerate(((a_ref, a_hbm), (b_ref, b_hbm), (c_ref, c_hbm)))
    ]
    for copy in copies:
        copy.start()
    for copy in copies:
        copy.wait()


def local(path_params, path_module, owner_of, outer_params, momentum):
    vmem = pl.BlockSpec(memory_space=pltpu.VMEM)
    hbm = pl.BlockSpec(memory_space=pl.ANY)
    shapes = (
        jax.ShapeDtypeStruct((1, R, 2048), F32),
        jax.ShapeDtypeStruct((1, R, 2048), F32),
        jax.ShapeDtypeStruct((2, R, 2048), BF16),
    )
    results = pl.pallas_call(
        kernel,
        out_shape=shapes,
        in_specs=[hbm] * 5,
        out_specs=(vmem, vmem, vmem),
        scratch_shapes=[
            pltpu.VMEM((1, 128), jnp.int32),
            pltpu.SMEM((MODULES,), jnp.int32),
            pltpu.VMEM((2, R, 2048), BF16),
            pltpu.VMEM((1, R, 2048), F32),
            pltpu.VMEM((1, R, 2048), F32),
            pltpu.VMEM((16 * N, 128), BF16),
            pltpu.VMEM((16 * N, 128), BF16),
            pltpu.VMEM((8 * N, 128), F32),
            pltpu.VMEM((8 * N, 128), F32),
            pltpu.VMEM((8 * N, 128), F32),
            pltpu.VMEM((R, 2048), F32),
            pltpu.VMEM((16 * N, 128), BF16),
            pltpu.VMEM((16 * N, 128), BF16),
            pltpu.VMEM((DP, 128), F32),
            pltpu.VMEM((N, 128), F32),
            pltpu.VMEM((8 * N, 1024), BF16),
            pltpu.VMEM((1024, 8 * N), BF16),
            pltpu.SemaphoreType.DMA((5,)),
            pltpu.SemaphoreType.DMA((7,)),
            pltpu.SemaphoreType.DMA((7,)),
        ],
        compiler_params=pltpu.CompilerParams(
            collective_id=0, has_side_effects=True, vmem_limit_bytes=53 << 20
        ),
    )(path_module.reshape(1, 128), owner_of, path_params, outer_params, momentum)
    return pl.pallas_call(
        write_out,
        out_shape=shapes,
        in_specs=[hbm] * 3,
        out_specs=(hbm,) * 3,
        scratch_shapes=[pltpu.SemaphoreType.DMA((3,))],
        compiler_params=pltpu.CompilerParams(vmem_limit_bytes=1 << 20),
    )(*results)


def solution(mesh):
    return jax.shard_map(
        local,
        mesh=mesh,
        in_specs=(P("path", None, "dp"), P(), P(), P("path", None, "dp"), P("path", None, "dp")),
        out_specs=(P("path", None, "dp"), P("path", None, "dp"), P("path", None, "dp")),
        check_vma=False,
    )
```

```python
import jax
import jax.numpy as jnp
from jax import lax
from jax.experimental import pallas as pl
from jax.experimental.pallas import tpu as pltpu
from jax.sharding import PartitionSpec as P

FF = 8192
R = 32
MODULES = 16
N = 64
DP = 4
MESH = pl.DeviceIdType.MESH
LINE = ((2, 1), (2, 0), (1, 1), (1, 0), (3, 1), (3, 0), (0, 1))
F32 = jnp.float32
BF16 = jnp.bfloat16


def zig(j, middle):
    return middle + (1 - 2 * lax.rem(j, 2)) * lax.div(j + 1, 2)


def peer(me, k):
    y, z, core = lax.div(me, 16), lax.rem(lax.div(me, 2), 8), lax.rem(me, 2)
    dy = zig(lax.div(k, 16), 2)
    dz = zig(lax.rem(lax.div(k, 2), 8), 4)
    dc = 1 - lax.rem(k, 2)
    return lax.rem(y + dy, 4) * 16 + lax.rem(z + dz, 8) * 2 + lax.rem(core + dc, 2)


def rows(index, count):
    return pl.ds(pl.multiple_of(index * count, count), count)


def tile(index):
    return (rows(lax.div(index, 16), 8), rows(lax.rem(index, 16), 128))


def kernel(
    module_hbm, owner_hbm, x_hbm, outer_hbm, mom_hbm,
    new_outer_ref, new_mom_ref, fresh_ref,
    module_ref, owner_ref, x_v, outer_v, mom_v, x_send, x_recv, outer_recv, mom_recv, mean_send, mean_slab,
    fresh_send, fresh_recv, dp_recv, vec_recv, weights, select,
    load_sem, send_sem, recv_sem, plane_sem,
):
    me = lax.axis_index("path")
    plane = lax.axis_index("dp")

    loads = [
        pltpu.make_async_copy(src, dst, load_sem.at[i])
        for i, (src, dst) in enumerate((
            (x_hbm, x_v), (outer_hbm, outer_v), (mom_hbm, mom_v),
            (module_hbm, module_ref), (owner_hbm, owner_ref),
        ))
    ]
    for load in loads:
        load.start()

    barrier = pltpu.get_barrier_semaphore()

    @pl.loop(0, N - 1, unroll=9)
    def _(k):
        pl.semaphore_signal(barrier, inc=1, device_id={"path": peer(me, k)}, device_id_type=MESH)

    for k in range(1, DP):
        to = {"dp": lax.rem(plane + k, DP)}
        pl.semaphore_signal(barrier, inc=1, device_id=to, device_id_type=MESH)

    loads[0].wait()
    for half in range(2):
        first = x_v[0, 16 * half : 16 * half + 16, :].astype(F32)
        second = x_v[1, 16 * half : 16 * half + 16, :].astype(F32)
        for part in range(2):
            both = jnp.concatenate(
                [first[8 * part : 8 * part + 8], second[8 * part : 8 * part + 8]], axis=0
            ).astype(BF16)
            for column in range(16):
                chunk = (2 * half + part) * 16 + column
                x_send[16 * chunk : 16 * chunk + 16, :] = both[:, 128 * column : 128 * column + 128]
    for load in loads[1:]:
        load.wait()

    pl.semaphore_wait(barrier, N - 1 + DP - 1)

    def send_all(stage, source, target):
        @pl.loop(0, N - 1, unroll=9)
        def _(k):
            to = peer(me, k)
            pltpu.make_async_remote_copy(
                src_ref=source(to), dst_ref=target, send_sem=send_sem.at[stage],
                recv_sem=recv_sem.at[stage], device_id={"path": to}, device_id_type=MESH,
            ).start()

    def send_early(stage, source, target):
        @pl.loop(0, N, unroll=8)
        def _(k):
            y, z, core = lax.div(me, 16), lax.rem(lax.div(me, 2), 8), lax.rem(me, 2)
            dy, dz, dc = lax.rem(lax.div(k, 8), 4), lax.rem(lax.div(k, 2), 4), lax.rem(k, 2)
            to = dy * 16 + (lax.div(k, 32) * 4 + lax.rem(z + dz, 4)) * 2 + lax.rem(core + dc, 2)

            @pl.when(to != me)
            def _():
                pltpu.make_async_remote_copy(
                    src_ref=source(to), dst_ref=target, send_sem=send_sem.at[stage],
                    recv_sem=recv_sem.at[stage], device_id={"path": to}, device_id_type=MESH,
                ).start()

    def wait(sem, ref, count):
        view = ref.at[pl.ds(0, count)]
        pltpu.make_async_copy(view, view, sem).wait()

    send_all(0, lambda to: x_send.at[rows(to, 16)], x_recv.at[rows(me, 16)])
    send_all(1, lambda to: outer_v.at[0].at[tile(to)], outer_recv.at[rows(me, 8)])
    send_all(2, lambda to: mom_v.at[0].at[tile(to)], mom_recv.at[rows(me, 8)])
    for k in range(1, DP):
        to = {"dp": lax.rem(plane + k, DP)}
        pl.semaphore_signal(plane_sem, inc=1, device_id=to, device_id_type=MESH)
    x_recv[rows(me, 16), :] = x_send[rows(me, 16), :]
    outer_recv[rows(me, 8), :] = outer_v[0, tile(me)[0], tile(me)[1]]
    mom_recv[rows(me, 8), :] = mom_v[0, tile(me)[0], tile(me)[1]]

    path_modules = jnp.broadcast_to(module_ref[...], (8, 128))
    slot_of_path = jnp.zeros((8, 128), jnp.int32)
    held_here = jnp.int32(0)
    for m in range(MODULES):
        owner = owner_ref[m]
        slot_of_path = jnp.where(path_modules == m, owner, slot_of_path)
        held_here = jnp.where(owner == me, 1, held_here)
    slot_of_path = slot_of_path.astype(F32)

    def iota(shape, axis):
        return lax.broadcasted_iota(jnp.int32, shape, axis)

    spread = (iota((128, 1024), 1) // 8 == iota((128, 1024), 0)).astype(F32).astype(BF16)
    across = jnp.dot(slot_of_path.astype(BF16), spread, preferred_element_type=F32)[0:1]
    shape = (N * 8, 1024)
    slot, row = (iota((N * 8, 1), 0) // 8).astype(F32), iota((N * 8, 1), 0) % 8
    hot = jnp.where((across == slot) & (iota((1, 1024), 1) % 8 == row), F32(1), F32(0))
    counts = jnp.sum(hot, axis=1, keepdims=True)
    weights[...] = hot.astype(BF16)
    down = jnp.sum(
        jnp.where(iota((1024, 128), 0) // 8 == iota((1024, 128), 1), slot_of_path[0:1], 0.0),
        axis=1, keepdims=True,
    )
    slot, row = (iota((1, N * 8), 1) // 8).astype(F32), iota((1, N * 8), 1) % 8
    select[...] = jnp.where(
        (down == slot) & (iota((1024, 1), 0) % 8 == row), F32(1), F32(0)
    ).astype(BF16)
    diagonal = iota((N * 8, 128), 0) // 8 == iota((N * 8, 128), 1)
    held = counts > 0.5
    divisor = jnp.maximum(counts, 1.0)

    wait(recv_sem.at[0], x_recv, 16 * (N - 1))
    sums = jnp.dot(weights[...], x_recv[...], preferred_element_type=F32)
    mean = sums / divisor
    mean_send[...] = mean
    wait(recv_sem.at[1], outer_recv, 8 * (N - 1))
    pseudo = jnp.where(held, outer_recv[...] - mean, 0.0)
    squares = jnp.sum(pseudo * pseudo, axis=1, keepdims=True)
    squares = jnp.sum(jnp.where(diagonal, squares, 0.0), axis=0, keepdims=True)

    core = lax.rem(me, 2)
    dp_recv[pl.ds(core, 1), :] = squares
    pltpu.make_async_remote_copy(
        src_ref=dp_recv.at[pl.ds(core, 1)], dst_ref=dp_recv.at[pl.ds(core, 1)],
        send_sem=send_sem.at[3], recv_sem=recv_sem.at[3],
        device_id={"path": me + 1 - 2 * core}, device_id_type=MESH,
    ).start()
    pl.semaphore_wait(plane_sem, DP - 1)
    wait(recv_sem.at[3], dp_recv, 1)
    chip = pl.ds(plane * (N // 2) + lax.div(me, 2), 1)
    vec_recv[chip, :] = dp_recv[0:1] + dp_recv[1:2]

    def to_chips(count, unroll, plane_of):
        @pl.loop(0, count, unroll=unroll)
        def _(k):
            y, z = lax.div(me, 16), lax.rem(lax.div(me, 2), 8)
            to = (
                lax.rem(y + zig(lax.rem(lax.div(k, 8), 4), 2), 4) * 16
                + lax.rem(z + zig(lax.rem(k, 8), 4), 8) * 2
                + core
            )
            pltpu.make_async_remote_copy(
                src_ref=vec_recv.at[chip], dst_ref=vec_recv.at[chip],
                send_sem=send_sem.at[5], recv_sem=recv_sem.at[5],
                device_id={"path": to, "dp": plane_of(k)}, device_id_type=MESH,
            ).start()

    to_chips(3 * N // 2, 4, lambda k: lax.rem(plane + zig(lax.div(k, 32), 2), DP))
    to_chips(N // 2 - 1, 1, lambda k: plane)

    send_all(4, lambda to: mean_send.at[rows(to, 8)], mean_slab.at[tile(me)])
    mean_slab[tile(me)[0], tile(me)[1]] = mean_send[rows(me, 8), :]
    wait(recv_sem.at[2], mom_recv, 8 * (N - 1))
    limit = 0.5 * (float(R * FF) ** 0.5)
    wait(recv_sem.at[5], vec_recv, 2 * N - 1)
    total = jnp.sum(vec_recv[...], axis=0, keepdims=True)
    factors = jnp.minimum(1.0, limit / jnp.sqrt(total + 1e-06))

    factor = jnp.sum(jnp.where(diagonal, factors, 0.0), axis=1, keepdims=True)
    grad = factor * pseudo
    velocity = 0.9 * mom_recv[...] + grad
    theta = outer_recv[...] - 0.7 * (0.9 * velocity + grad)
    fresh_send[...] = jnp.dot(
        select[...], theta.astype(BF16), preferred_element_type=F32
    ).astype(BF16)
    send_early(6, lambda to: fresh_send.at[rows(to, 16)], fresh_recv.at[rows(me, 16)])
    fresh_recv[rows(me, 16), :] = fresh_send[rows(me, 16), :]

    held_slot = held_here > 0
    own_factor = jnp.sum(
        jnp.where(iota((1, 128), 1) == me, factors, 0.0), axis=1, keepdims=True
    )
    wait(recv_sem.at[4], mean_send, 8 * (N - 1))
    outer, mom = outer_v[0], mom_v[0]
    grad = own_factor * (outer - mean_slab[...])
    velocity = 0.9 * mom + grad
    theta = outer - 0.7 * (0.9 * velocity + grad)
    new_outer_ref[0] = jnp.where(held_slot, theta, outer)
    new_mom_ref[0] = jnp.where(held_slot, velocity, mom)

    wait(recv_sem.at[6], fresh_recv, 16 * (N - 1))
    for half in range(2):
        for column in range(16):
            top = fresh_recv[16 * (32 * half + column) : 16 * (32 * half + column) + 16, :].astype(F32)
            low = 16 * (32 * half + 16 + column)
            bottom = fresh_recv[low : low + 16, :].astype(F32)
            for path in range(2):
                fresh_ref[path, 16 * half : 16 * half + 16, 128 * column : 128 * column + 128] = (
                    jnp.concatenate(
                        [top[8 * path : 8 * path + 8], bottom[8 * path : 8 * path + 8]], axis=0
                    ).astype(BF16)
                )

    wait(send_sem.at[0], x_send, 16 * (N - 1))
    wait(send_sem.at[1], outer_recv, 8 * (N - 1))
    wait(send_sem.at[2], mom_recv, 8 * (N - 1))
    wait(send_sem.at[3], dp_recv, 1)
    wait(send_sem.at[4], mean_send, 8 * (N - 1))
    wait(send_sem.at[5], vec_recv, 2 * N - 1)
    wait(send_sem.at[6], fresh_send, 16 * (N - 1))


def write_out(a_ref, b_ref, c_ref, a_hbm, b_hbm, c_hbm, sem):
    copies = [
        pltpu.make_async_copy(src, dst, sem.at[i])
        for i, (src, dst) in enumerate(((a_ref, a_hbm), (b_ref, b_hbm), (c_ref, c_hbm)))
    ]
    for copy in copies:
        copy.start()
    for copy in copies:
        copy.wait()


def local(path_params, path_module, owner_of, outer_params, momentum):
    vmem = pl.BlockSpec(memory_space=pltpu.VMEM)
    hbm = pl.BlockSpec(memory_space=pl.ANY)
    shapes = (
        jax.ShapeDtypeStruct((1, R, 2048), F32),
        jax.ShapeDtypeStruct((1, R, 2048), F32),
        jax.ShapeDtypeStruct((2, R, 2048), BF16),
    )
    results = pl.pallas_call(
        kernel,
        out_shape=shapes,
        in_specs=[hbm] * 5,
        out_specs=(vmem, vmem, vmem),
        scratch_shapes=[
            pltpu.VMEM((1, 128), jnp.int32),
            pltpu.SMEM((MODULES,), jnp.int32),
            pltpu.VMEM((2, R, 2048), BF16),
            pltpu.VMEM((1, R, 2048), F32),
            pltpu.VMEM((1, R, 2048), F32),
            pltpu.VMEM((16 * N, 128), BF16),
            pltpu.VMEM((16 * N, 128), BF16),
            pltpu.VMEM((8 * N, 128), F32),
            pltpu.VMEM((8 * N, 128), F32),
            pltpu.VMEM((8 * N, 128), F32),
            pltpu.VMEM((R, 2048), F32),
            pltpu.VMEM((16 * N, 128), BF16),
            pltpu.VMEM((16 * N, 128), BF16),
            pltpu.VMEM((2, 128), F32),
            pltpu.VMEM((2 * N, 128), F32),
            pltpu.VMEM((8 * N, 1024), BF16),
            pltpu.VMEM((1024, 8 * N), BF16),
            pltpu.SemaphoreType.DMA((5,)),
            pltpu.SemaphoreType.DMA((7,)),
            pltpu.SemaphoreType.DMA((7,)),
            pltpu.SemaphoreType.REGULAR,
        ],
        compiler_params=pltpu.CompilerParams(
            collective_id=0, has_side_effects=True, vmem_limit_bytes=53 << 20
        ),
    )(path_module.reshape(1, 128), owner_of, path_params, outer_params, momentum)
    return pl.pallas_call(
        write_out,
        out_shape=shapes,
        in_specs=[hbm] * 3,
        out_specs=(hbm,) * 3,
        scratch_shapes=[pltpu.SemaphoreType.DMA((3,))],
        compiler_params=pltpu.CompilerParams(vmem_limit_bytes=1 << 20),
    )(*results)


def solution(mesh):
    return jax.shard_map(
        local,
        mesh=mesh,
        in_specs=(P("path", None, "dp"), P(), P(), P("path", None, "dp"), P("path", None, "dp")),
        out_specs=(P("path", None, "dp"), P("path", None, "dp"), P("path", None, "dp")),
        check_vma=False,
    )
```

```python
import jax
import jax.numpy as jnp
from jax import lax
from jax.experimental import pallas as pl
from jax.experimental.pallas import tpu as pltpu
from jax.sharding import PartitionSpec as P

FF = 8192
R = 32
MODULES = 16
N = 64
DP = 4
MESH = pl.DeviceIdType.MESH
LINE = ((2, 1), (2, 0), (1, 1), (1, 0), (3, 1), (3, 0), (0, 1))
F32 = jnp.float32
BF16 = jnp.bfloat16


def zig(j, middle):
    return middle + (1 - 2 * lax.rem(j, 2)) * lax.div(j + 1, 2)


def peer(me, k):
    y, z, core = lax.div(me, 16), lax.rem(lax.div(me, 2), 8), lax.rem(me, 2)
    dy = zig(lax.div(k, 16), 2)
    dz = zig(lax.rem(lax.div(k, 2), 8), 4)
    dc = 1 - lax.rem(k, 2)
    return lax.rem(y + dy, 4) * 16 + lax.rem(z + dz, 8) * 2 + lax.rem(core + dc, 2)


def rows(index, count):
    return pl.ds(pl.multiple_of(index * count, count), count)


def tile(index):
    return (rows(lax.div(index, 16), 8), rows(lax.rem(index, 16), 128))


def kernel(
    module_hbm, owner_hbm, x_hbm, outer_hbm, mom_hbm,
    new_outer_ref, new_mom_ref, fresh_ref,
    module_ref, owner_ref, x_v, outer_v, mom_v, x_send, x_recv, outer_recv, mom_recv, mean_send, mean_slab,
    fresh_send, fresh_recv, dp_recv, vec_recv, weights, select,
    load_sem, send_sem, recv_sem, plane_sem,
):
    me = lax.axis_index("path")
    plane = lax.axis_index("dp")

    loads = [
        pltpu.make_async_copy(src, dst, load_sem.at[i])
        for i, (src, dst) in enumerate((
            (x_hbm, x_v), (outer_hbm, outer_v), (mom_hbm, mom_v),
            (module_hbm, module_ref), (owner_hbm, owner_ref),
        ))
    ]
    for load in loads:
        load.start()

    barrier = pltpu.get_barrier_semaphore()

    @pl.loop(0, N - 1, unroll=21)
    def _(k):
        pl.semaphore_signal(barrier, inc=1, device_id={"path": peer(me, k)}, device_id_type=MESH)

    for k in range(1, DP):
        to = {"dp": lax.rem(plane + k, DP)}
        pl.semaphore_signal(barrier, inc=1, device_id=to, device_id_type=MESH)

    loads[0].wait()
    for half in range(2):
        first = x_v[0, 16 * half : 16 * half + 16, :].astype(F32)
        second = x_v[1, 16 * half : 16 * half + 16, :].astype(F32)
        for part in range(2):
            both = jnp.concatenate(
                [first[8 * part : 8 * part + 8], second[8 * part : 8 * part + 8]], axis=0
            ).astype(BF16)
            for column in range(16):
                chunk = (2 * half + part) * 16 + column
                x_send[16 * chunk : 16 * chunk + 16, :] = both[:, 128 * column : 128 * column + 128]
    for load in loads[1:]:
        load.wait()

    pl.semaphore_wait(barrier, N - 1 + DP - 1)

    def send_all(stage, source, target):
        @pl.loop(0, N - 1, unroll=21)
        def _(k):
            to = peer(me, k)
            pltpu.make_async_remote_copy(
                src_ref=source(to), dst_ref=target, send_sem=send_sem.at[stage],
                recv_sem=recv_sem.at[stage], device_id={"path": to}, device_id_type=MESH,
            ).start()

    def send_early(stage, source, target, first=0, last=N):
        @pl.loop(first, last, unroll=8)
        def _(k):
            y, z, core = lax.div(me, 16), lax.rem(lax.div(me, 2), 8), lax.rem(me, 2)
            dy, dz, dc = lax.rem(lax.div(k, 8), 4), lax.rem(lax.div(k, 2), 4), lax.rem(k, 2)
            to = dy * 16 + (lax.div(k, 32) * 4 + lax.rem(z + dz, 4)) * 2 + lax.rem(core + dc, 2)

            @pl.when(to != me)
            def _():
                pltpu.make_async_remote_copy(
                    src_ref=source(to), dst_ref=target, send_sem=send_sem.at[stage],
                    recv_sem=recv_sem.at[stage], device_id={"path": to}, device_id_type=MESH,
                ).start()

    def wait(sem, ref, count):
        view = ref.at[pl.ds(0, count)]
        pltpu.make_async_copy(view, view, sem).wait()

    send_all(0, lambda to: x_send.at[rows(to, 16)], x_recv.at[rows(me, 16)])
    send_all(1, lambda to: outer_v.at[0].at[tile(to)], outer_recv.at[rows(me, 8)])
    send_all(2, lambda to: mom_v.at[0].at[tile(to)], mom_recv.at[rows(me, 8)])
    for k in range(1, DP):
        to = {"dp": lax.rem(plane + k, DP)}
        pl.semaphore_signal(plane_sem, inc=1, device_id=to, device_id_type=MESH)
    x_recv[rows(me, 16), :] = x_send[rows(me, 16), :]
    outer_recv[rows(me, 8), :] = outer_v[0, tile(me)[0], tile(me)[1]]
    mom_recv[rows(me, 8), :] = mom_v[0, tile(me)[0], tile(me)[1]]

    path_modules = jnp.broadcast_to(module_ref[...], (8, 128))
    slot_of_path = jnp.zeros((8, 128), jnp.int32)
    held_here = jnp.int32(0)
    for m in range(MODULES):
        owner = owner_ref[m]
        slot_of_path = jnp.where(path_modules == m, owner, slot_of_path)
        held_here = jnp.where(owner == me, 1, held_here)
    slot_of_path = slot_of_path.astype(F32)

    def iota(shape, axis):
        return lax.broadcasted_iota(jnp.int32, shape, axis)

    spread = (iota((128, 1024), 1) // 8 == iota((128, 1024), 0)).astype(F32).astype(BF16)
    across = jnp.dot(slot_of_path.astype(BF16), spread, preferred_element_type=F32)[0:1]
    shape = (N * 8, 1024)
    slot, row = (iota((N * 8, 1), 0) // 8).astype(F32), iota((N * 8, 1), 0) % 8
    hot = jnp.where((across == slot) & (iota((1, 1024), 1) % 8 == row), F32(1), F32(0))
    counts = jnp.sum(hot, axis=1, keepdims=True)
    weights[...] = hot.astype(BF16)
    down = jnp.sum(
        jnp.where(iota((1024, 128), 0) // 8 == iota((1024, 128), 1), slot_of_path[0:1], 0.0),
        axis=1, keepdims=True,
    )
    slot, row = (iota((1, N * 8), 1) // 8).astype(F32), iota((1, N * 8), 1) % 8
    select[...] = jnp.where(
        (down == slot) & (iota((1024, 1), 0) % 8 == row), F32(1), F32(0)
    ).astype(BF16)
    diagonal = iota((N * 8, 128), 0) // 8 == iota((N * 8, 128), 1)
    held = counts > 0.5
    divisor = jnp.maximum(counts, 1.0)

    wait(recv_sem.at[0], x_recv, 16 * (N - 1))
    sums = jnp.dot(weights[...], x_recv[...], preferred_element_type=F32)
    mean = sums / divisor
    mean_send[...] = mean
    wait(recv_sem.at[1], outer_recv, 8 * (N - 1))
    pseudo = jnp.where(held, outer_recv[...] - mean, 0.0)
    squares = jnp.sum(pseudo * pseudo, axis=1, keepdims=True)
    squares = jnp.sum(jnp.where(diagonal, squares, 0.0), axis=0, keepdims=True)

    core = lax.rem(me, 2)
    dp_recv[pl.ds(core, 1), :] = squares
    pltpu.make_async_remote_copy(
        src_ref=dp_recv.at[pl.ds(core, 1)], dst_ref=dp_recv.at[pl.ds(core, 1)],
        send_sem=send_sem.at[3], recv_sem=recv_sem.at[3],
        device_id={"path": me + 1 - 2 * core}, device_id_type=MESH,
    ).start()
    pl.semaphore_wait(plane_sem, DP - 1)
    wait(recv_sem.at[3], dp_recv, 1)
    chip = pl.ds(plane * (N // 2) + lax.div(me, 2), 1)
    vec_recv[chip, :] = dp_recv[0:1] + dp_recv[1:2]

    def to_chips(count, unroll, plane_of):
        @pl.loop(0, count, unroll=unroll)
        def _(k):
            y, z = lax.div(me, 16), lax.rem(lax.div(me, 2), 8)
            to = (
                lax.rem(y + zig(lax.rem(lax.div(k, 8), 4), 2), 4) * 16
                + lax.rem(z + zig(lax.rem(k, 8), 4), 8) * 2
                + core
            )
            pltpu.make_async_remote_copy(
                src_ref=vec_recv.at[chip], dst_ref=vec_recv.at[chip],
                send_sem=send_sem.at[5], recv_sem=recv_sem.at[5],
                device_id={"path": to, "dp": plane_of(k)}, device_id_type=MESH,
            ).start()

    to_chips(3 * N // 2, 32, lambda k: lax.rem(plane + zig(lax.div(k, 32), 2), DP))
    to_chips(N // 2 - 1, 31, lambda k: plane)

    send_early(4, lambda to: mean_send.at[rows(to, 8)], mean_slab.at[tile(me)], 0, N)
    mean_slab[tile(me)[0], tile(me)[1]] = mean_send[rows(me, 8), :]
    wait(recv_sem.at[2], mom_recv, 8 * (N - 1))
    limit = 0.5 * (float(R * FF) ** 0.5)
    wait(recv_sem.at[5], vec_recv, 2 * N - 1)
    total = jnp.sum(vec_recv[...], axis=0, keepdims=True)
    factors = jnp.minimum(1.0, limit / jnp.sqrt(total + 1e-06))

    factor = jnp.sum(jnp.where(diagonal, factors, 0.0), axis=1, keepdims=True)
    grad = factor * pseudo
    velocity = 0.9 * mom_recv[...] + grad
    theta = outer_recv[...] - 0.7 * (0.9 * velocity + grad)
    fresh_send[...] = jnp.dot(
        select[...], theta.astype(BF16), preferred_element_type=F32
    ).astype(BF16)
    send_early(6, lambda to: fresh_send.at[rows(to, 16)], fresh_recv.at[rows(me, 16)])
    fresh_recv[rows(me, 16), :] = fresh_send[rows(me, 16), :]

    held_slot = held_here > 0
    own_factor = jnp.sum(
        jnp.where(iota((1, 128), 1) == me, factors, 0.0), axis=1, keepdims=True
    )
    wait(recv_sem.at[4], mean_send, 8 * (N - 1))
    outer, mom = outer_v[0], mom_v[0]
    grad = own_factor * (outer - mean_slab[...])
    velocity = 0.9 * mom + grad
    theta = outer - 0.7 * (0.9 * velocity + grad)
    new_outer_ref[0] = jnp.where(held_slot, theta, outer)
    new_mom_ref[0] = jnp.where(held_slot, velocity, mom)

    wait(recv_sem.at[6], fresh_recv, 16 * (N - 1))
    for half in range(2):
        for column in range(16):
            top = fresh_recv[16 * (32 * half + column) : 16 * (32 * half + column) + 16, :].astype(F32)
            low = 16 * (32 * half + 16 + column)
            bottom = fresh_recv[low : low + 16, :].astype(F32)
            for path in range(2):
                fresh_ref[path, 16 * half : 16 * half + 16, 128 * column : 128 * column + 128] = (
                    jnp.concatenate(
                        [top[8 * path : 8 * path + 8], bottom[8 * path : 8 * path + 8]], axis=0
                    ).astype(BF16)
                )

    wait(send_sem.at[0], x_send, 16 * (N - 1))
    wait(send_sem.at[1], outer_recv, 8 * (N - 1))
    wait(send_sem.at[2], mom_recv, 8 * (N - 1))
    wait(send_sem.at[3], dp_recv, 1)
    wait(send_sem.at[4], mean_send, 8 * (N - 1))
    wait(send_sem.at[5], vec_recv, 2 * N - 1)
    wait(send_sem.at[6], fresh_send, 16 * (N - 1))


def write_out(a_ref, b_ref, c_ref, a_hbm, b_hbm, c_hbm, sem):
    copies = [
        pltpu.make_async_copy(src, dst, sem.at[i])
        for i, (src, dst) in enumerate(((a_ref, a_hbm), (b_ref, b_hbm), (c_ref, c_hbm)))
    ]
    for copy in copies:
        copy.start()
    for copy in copies:
        copy.wait()


def local(path_params, path_module, owner_of, outer_params, momentum):
    vmem = pl.BlockSpec(memory_space=pltpu.VMEM)
    hbm = pl.BlockSpec(memory_space=pl.ANY)
    shapes = (
        jax.ShapeDtypeStruct((1, R, 2048), F32),
        jax.ShapeDtypeStruct((1, R, 2048), F32),
        jax.ShapeDtypeStruct((2, R, 2048), BF16),
    )
    results = pl.pallas_call(
        kernel,
        out_shape=shapes,
        in_specs=[hbm] * 5,
        out_specs=(vmem, vmem, vmem),
        scratch_shapes=[
            pltpu.VMEM((1, 128), jnp.int32),
            pltpu.SMEM((MODULES,), jnp.int32),
            pltpu.VMEM((2, R, 2048), BF16),
            pltpu.VMEM((1, R, 2048), F32),
            pltpu.VMEM((1, R, 2048), F32),
            pltpu.VMEM((16 * N, 128), BF16),
            pltpu.VMEM((16 * N, 128), BF16),
            pltpu.VMEM((8 * N, 128), F32),
            pltpu.VMEM((8 * N, 128), F32),
            pltpu.VMEM((8 * N, 128), F32),
            pltpu.VMEM((R, 2048), F32),
            pltpu.VMEM((16 * N, 128), BF16),
            pltpu.VMEM((16 * N, 128), BF16),
            pltpu.VMEM((2, 128), F32),
            pltpu.VMEM((2 * N, 128), F32),
            pltpu.VMEM((8 * N, 1024), BF16),
            pltpu.VMEM((1024, 8 * N), BF16),
            pltpu.SemaphoreType.DMA((5,)),
            pltpu.SemaphoreType.DMA((7,)),
            pltpu.SemaphoreType.DMA((7,)),
            pltpu.SemaphoreType.REGULAR,
        ],
        compiler_params=pltpu.CompilerParams(
            collective_id=0, has_side_effects=True, vmem_limit_bytes=53 << 20
        ),
    )(path_module.reshape(1, 128), owner_of, path_params, outer_params, momentum)
    return pl.pallas_call(
        write_out,
        out_shape=shapes,
        in_specs=[hbm] * 3,
        out_specs=(hbm,) * 3,
        scratch_shapes=[pltpu.SemaphoreType.DMA((3,))],
        compiler_params=pltpu.CompilerParams(vmem_limit_bytes=1 << 20),
    )(*results)


def solution(mesh):
    return jax.shard_map(
        local,
        mesh=mesh,
        in_specs=(P("path", None, "dp"), P(), P(), P("path", None, "dp"), P("path", None, "dp")),
        out_specs=(P("path", None, "dp"), P("path", None, "dp"), P("path", None, "dp")),
        check_vma=False,
    )
```
